32 devices in a mesh: dc: 16 (over z, y, x), kv: 2 (over core).
Axes of the slice: x: 2, y: 2, z: 4, core: 2. Of those that a mesh axis runs over, the one named last changes fastest.
Arguments:
- queries: bfloat16 [5120, 5120], P('dc', 'kv'), may hold values from -41 to 41
- keys: bfloat16 [5120, 1024], P('dc', 'kv'), may hold values from -4 to 4
- values: bfloat16 [5120, 1024], P('dc', 'kv'), may hold values from -6 to 6
- output_gradient: bfloat16 [5120, 5120], P('dc', 'kv'), may hold values from -6 to 6
- segment_ids: int32 [5120], P('dc'), may hold values from 0 to 7, as said below
- w_query: bfloat16 [5120, 5120], P(None, 'kv'), may hold values from -0.078125 to 0.078125
- key_weight_matrix: bfloat16 [5120, 1024], P(None, 'kv'), may hold values from -0.078125 to 0.078125
- value_weight_matrix: bfloat16 [5120, 1024], P(None, 'kv'), may hold values from -0.078125 to 0.078125
Outputs:
- query_grad: bfloat16 [5120, 5120], P('dc', 'kv')
- key_grad: bfloat16 [5120, 1024], P('dc', 'kv')
- value_grad: bfloat16 [5120, 1024], P('dc', 'kv')
- input_grad: bfloat16 [5120, 5120], P('dc', 'kv')
The draws below stay inside these ranges and needn't reach their ends.
Inputs may be any that keep to these rules, and one draw needn't show every extreme that they name: `segment_ids`: segment ids never fall along the tokens; every document has 1 to 2241 tokens and one has exactly 2241.
All inputs are finite; a program needn't handle non-finite values.
Results may differ from the reference program's by a relative error of at most 0.0065.
Values may be sent and summed in bfloat16 or wider, within the bound.
A program may use at most 448 MiB of HBM per device.

```python
import jax
import jax.numpy as jnp
from jax import lax

MODEL_WIDTH = 5120
QUERY_HEAD_COUNT = 40
KEY_VALUE_HEADS = 8
HEAD_SIZE = 128
TOKENS_PER_SHARD = 320
REACH = 8
TOKEN_TOTAL = 5120
MOST = 2241
DOCS = 8
N_DC = 16
N_KV = 2


def joint_draw(key):
    base = jax.random.fold_in(key, 11)
    query_key, key_random_seed = jax.random.split(base, 2)
    query_base = jnp.clip(jax.random.normal(query_key, (TOKEN_TOTAL, QUERY_HEAD_COUNT * HEAD_SIZE), jnp.float32), -4.0, 4.0)
    key_offset = jnp.clip(jax.random.normal(key_random_seed, (TOKEN_TOTAL, KEY_VALUE_HEADS * HEAD_SIZE), jnp.float32), -4.0, 4.0)
    return (query_base, key_offset)


def draw_queries(key, part):
    return joint_draw(key)[0].astype(jnp.bfloat16)


def draw_keys(key, part):
    return joint_draw(key)[1].astype(jnp.bfloat16)


def draw_segment_ids(key, part):
    front_tokens = TOKEN_TOTAL - MOST
    stride = front_tokens // (DOCS - 1)
    jitter_reach = stride // 3
    inner = jnp.arange(1, DOCS - 1, dtype=jnp.int32)
    jitter = jax.random.randint(jax.random.fold_in(key, 29), (DOCS - 2,), -jitter_reach, jitter_reach + 1, jnp.int32)
    inner_cuts = inner * stride + jitter
    cuts = jnp.concatenate([inner_cuts, jnp.full((1,), front_tokens, jnp.int32)])
    positions = jnp.arange(TOKEN_TOTAL, dtype=jnp.int32)
    return jnp.sum((positions[:, None] >= cuts[None, :]).astype(jnp.int32), axis=1).astype(jnp.int32)


def levels(own_key, dims, cuts, smallest, top_value):
    loudness = 1.0
    for dim, blocks in cuts:
        draws = jax.random.uniform(jax.random.fold_in(jax.random.fold_in(own_key, 6), dim), (blocks,), jnp.float32, smallest / len(cuts), top_value / len(cuts))
        loudness = loudness * jnp.repeat(jnp.exp(draws), dims[dim] // blocks).reshape((-1,) + (1,) * (len(dims) - 1 - dim))
    return loudness


def gaussian(key, shape, scale, bound, shards=(), kind=jnp.bfloat16):
    values = scale * jax.random.normal(key, shape, jnp.float32)
    if shards:
        values = values * levels(key, shape, shards, -0.22, 0.18)
    return jnp.clip(values, -bound, bound).astype(kind)


def setup_inputs(seed: int = 0) -> dict:
    splits = jax.random.split(jax.random.key(seed), 9)
    queries = draw_queries(jax.random.fold_in(splits[8], 71), 0)
    keys = draw_keys(jax.random.fold_in(splits[8], 71), 0)
    values = gaussian(splits[2], (TOKEN_TOTAL, KEY_VALUE_HEADS * HEAD_SIZE), 1.0, 6.0, ((0, 16), (1, 2)))
    output_gradient = gaussian(splits[3], (TOKEN_TOTAL, QUERY_HEAD_COUNT * HEAD_SIZE), 1.0, 6.0, ((0, 16), (1, 2)))
    segment_ids = draw_segment_ids(jax.random.fold_in(splits[8], 71), 0)
    w_query = gaussian(splits[5], (MODEL_WIDTH, QUERY_HEAD_COUNT * HEAD_SIZE), MODEL_WIDTH ** -0.5, 0.078125, ((1, 2),))
    key_weight_matrix = gaussian(splits[6], (MODEL_WIDTH, KEY_VALUE_HEADS * HEAD_SIZE), MODEL_WIDTH ** -0.5, 0.078125, ((1, 2),))
    value_weight_matrix = gaussian(splits[7], (MODEL_WIDTH, KEY_VALUE_HEADS * HEAD_SIZE), MODEL_WIDTH ** -0.5, 0.078125, ((1, 2),))
    return {"queries": queries, "keys": keys, "values": values, "output_gradient": output_gradient, "segment_ids": segment_ids, "w_query": w_query, "key_weight_matrix": key_weight_matrix, "value_weight_matrix": value_weight_matrix}


def reference(queries, keys, values, output_gradient, segment_ids, w_query, key_weight_matrix, value_weight_matrix):
    group_width = QUERY_HEAD_COUNT // KEY_VALUE_HEADS
    softmax_scale = HEAD_SIZE ** -0.5
    padding_extent = (REACH - 1) * TOKENS_PER_SHARD
    attention_span = REACH * TOKENS_PER_SHARD
    padded_keys = jnp.concatenate([jnp.zeros((padding_extent, KEY_VALUE_HEADS * HEAD_SIZE), jnp.bfloat16), keys], axis=0)
    padded_values = jnp.concatenate([jnp.zeros((padding_extent, KEY_VALUE_HEADS * HEAD_SIZE), jnp.bfloat16), values], axis=0)
    segs_padded = jnp.concatenate([jnp.full((padding_extent,), -1, jnp.int32), segment_ids], axis=0)

    def one_block(carry, block):
        key_acc, value_acc = carry
        leading_flag = (block * TOKENS_PER_SHARD).astype(jnp.int32)
        query_block = lax.dynamic_slice_in_dim(queries, leading_flag, TOKENS_PER_SHARD, 0).astype(jnp.float32).reshape(TOKENS_PER_SHARD, KEY_VALUE_HEADS, group_width, HEAD_SIZE)
        gradient_block = lax.dynamic_slice_in_dim(output_gradient, leading_flag, TOKENS_PER_SHARD, 0).astype(jnp.float32).reshape(TOKENS_PER_SHARD, KEY_VALUE_HEADS, group_width, HEAD_SIZE)
        key_span_rows = lax.dynamic_slice_in_dim(padded_keys, leading_flag, attention_span, 0).astype(jnp.float32).reshape(attention_span, KEY_VALUE_HEADS, HEAD_SIZE)
        value_span_rows = lax.dynamic_slice_in_dim(padded_values, leading_flag, attention_span, 0).astype(jnp.float32).reshape(attention_span, KEY_VALUE_HEADS, HEAD_SIZE)
        seg_query = lax.dynamic_slice_in_dim(segment_ids, leading_flag, TOKENS_PER_SHARD, 0)
        seg_key = lax.dynamic_slice_in_dim(segs_padded, leading_flag, attention_span, 0)
        pos_query = leading_flag + jnp.arange(TOKENS_PER_SHARD, dtype=jnp.int32)
        pos_key = leading_flag - padding_extent + jnp.arange(attention_span, dtype=jnp.int32)
        allowed = (seg_key[None, :] == seg_query[:, None]) & (pos_key[None, :] <= pos_query[:, None])
        scores = jnp.einsum('tkgd,skd->kgts', query_block, key_span_rows) * softmax_scale
        top = jnp.max(jnp.where(allowed, scores, -jnp.inf), axis=-1, keepdims=True)
        expo = jnp.where(allowed, jnp.exp(scores - top), 0.0)
        probs = expo / jnp.sum(expo, axis=-1, keepdims=True)
        probability_narrow = lax.optimization_barrier(probs.astype(jnp.bfloat16)).astype(jnp.float32)
        dprobs = jnp.einsum('tkgd,skd->kgts', gradient_block, value_span_rows)
        delta = jnp.sum(probs * dprobs, axis=-1, keepdims=True)
        score_gradient = lax.optimization_barrier((probs * (dprobs - delta)).astype(jnp.bfloat16)).astype(jnp.float32)
        query_part = (jnp.einsum('kgts,skd->tkgd', score_gradient, key_span_rows) * softmax_scale).astype(jnp.bfloat16).reshape(TOKENS_PER_SHARD, QUERY_HEAD_COUNT * HEAD_SIZE)
        key_portion = (jnp.einsum('qwuh,uqwb->hqb', score_gradient, query_block) * softmax_scale).reshape(attention_span, KEY_VALUE_HEADS * HEAD_SIZE)
        value_portion = jnp.einsum('qwuh,uqwb->hqb', probability_narrow, gradient_block).reshape(attention_span, KEY_VALUE_HEADS * HEAD_SIZE)
        key_acc = lax.dynamic_update_slice_in_dim(key_acc, lax.dynamic_slice_in_dim(key_acc, leading_flag, attention_span, 0) + key_portion, leading_flag, 0)
        value_acc = lax.dynamic_update_slice_in_dim(value_acc, lax.dynamic_slice_in_dim(value_acc, leading_flag, attention_span, 0) + value_portion, leading_flag, 0)
        return (key_acc, value_acc), query_part

    initial_accumulator = jnp.zeros((TOKEN_TOTAL + padding_extent, KEY_VALUE_HEADS * HEAD_SIZE), jnp.float32)
    (key_acc, value_acc), query_parts = lax.scan(one_block, (initial_accumulator, initial_accumulator), jnp.arange(N_DC, dtype=jnp.int32))
    query_grad = query_parts.reshape(TOKEN_TOTAL, QUERY_HEAD_COUNT * HEAD_SIZE)
    key_grad = key_acc[padding_extent:].astype(jnp.bfloat16)
    value_grad = value_acc[padding_extent:].astype(jnp.bfloat16)
    query_cols = QUERY_HEAD_COUNT * HEAD_SIZE // N_KV
    key_value_columns = KEY_VALUE_HEADS * HEAD_SIZE // N_KV
    total = jnp.zeros((TOKEN_TOTAL, MODEL_WIDTH), jnp.float32)
    for member in range(N_KV):
        qsl = slice(member * query_cols, (member + 1) * query_cols)
        ksl = slice(member * key_value_columns, (member + 1) * key_value_columns)
        term = jnp.dot(query_grad[:, qsl], w_query[:, qsl].T, preferred_element_type=jnp.float32)
        term = term + jnp.dot(key_grad[:, ksl], key_weight_matrix[:, ksl].T, preferred_element_type=jnp.float32)
        term = term + jnp.dot(value_grad[:, ksl], value_weight_matrix[:, ksl].T, preferred_element_type=jnp.float32)
        total = total + lax.optimization_barrier(term.astype(jnp.bfloat16)).astype(jnp.float32)
    return query_grad, key_grad, value_grad, total.astype(jnp.bfloat16)
```

```python
import functools

import jax
import jax.numpy as jnp
from jax import lax
from jax.experimental import pallas as pl
from jax.experimental.pallas import tpu as pltpu
from jax.sharding import PartitionSpec as P

QUERY_HEAD_COUNT = 40
KEY_VALUE_HEADS = 8
HEAD_SIZE = 128
GROUP_WIDTH = QUERY_HEAD_COUNT // KEY_VALUE_HEADS
REACH = 8
PLANE = 4
HEAD_CHUNKS = 2
SCALE = HEAD_SIZE ** (-0.5)
LOG2E = 1.4426950408889634
LOW = -1e30


def attention_kernel(
    info_ref, rows_ref, q_ref, g_ref, kv_ref, dq_ref, dkv_ref, s_ref, dp_ref, p_ref, ds_ref, stat_ref
):
    tok = kv_ref.shape[1]
    wide = q_ref.shape[0]
    lanes = []
    at = 0
    while at < wide:
        size = 512 if wide - at >= 1024 else wide - at
        lanes.append((at, size))
        at += size
    nt = (((1,), (1,)), ((), ()))
    tn = (((0,), (0,)), ((), ()))
    first_start = info_ref[REACH]
    last_start = info_ref[REACH + 1]

    stat_ref[0:1, :] = jnp.full((1, wide), LOW, jnp.float32)
    stat_ref[1:3, :] = jnp.zeros((2, wide), jnp.float32)

    def needed(slot):
        base = info_ref[slot]
        return (base >= 0) & (base + tok > first_start)

    def gather_stats(slot, masked):
        base = info_ref[slot]
        keys = kv_ref[slot, :, :HEAD_SIZE]
        values = kv_ref[slot, :, HEAD_SIZE:]
        for lo, size in lanes:
            cols = slice(lo, lo + size)
            s = lax.dot_general(
                keys, q_ref[cols, :], nt, preferred_element_type=jnp.float32
            ) * (SCALE * LOG2E)
            dp = lax.dot_general(values, g_ref[cols, :], nt, preferred_element_type=jnp.float32)
            if masked:
                pos = base + lax.broadcasted_iota(jnp.int32, (tok, size), 0)
                ok = (pos >= rows_ref[0:1, cols]) & (pos <= rows_ref[1:2, cols])
                s = jnp.where(ok, s, LOW)
            s_ref[slot, :, cols] = s
            dp_ref[slot, :, cols] = dp
            old = stat_ref[0:1, cols]
            new = jnp.maximum(old, jnp.max(s, axis=0, keepdims=True))
            fade = jnp.exp2(old - new)
            e = jnp.exp2(s - new)
            stat_ref[0:1, cols] = new
            stat_ref[1:2, cols] = stat_ref[1:2, cols] * fade + jnp.sum(e, axis=0, keepdims=True)
            stat_ref[2:3, cols] = stat_ref[2:3, cols] * fade + jnp.sum(
                e * dp, axis=0, keepdims=True
            )

    @pl.loop(0, REACH)
    def _(slot):
        whole = (slot > 0) & (info_ref[slot] >= last_start)

        @pl.when(needed(slot) & whole)
        def _():
            gather_stats(slot, False)

        @pl.when(needed(slot) & jnp.logical_not(whole))
        def _():
            gather_stats(slot, True)

    total = stat_ref[1:2, :]
    stat_ref[2:3, :] = stat_ref[2:3, :] / total
    stat_ref[0:1, :] = stat_ref[0:1, :] + jnp.log2(total)
    dq_ref[...] = jnp.zeros_like(dq_ref)

    @pl.loop(0, REACH)
    def _(slot):
        need = needed(slot)

        @pl.when(need)
        def _():
            keys = kv_ref[slot, :, :HEAD_SIZE]
            for lo, size in lanes:
                cols = slice(lo, lo + size)
                p = jnp.exp2(s_ref[slot, :, cols] - stat_ref[0:1, cols])
                p_ref[:, cols] = p.astype(jnp.bfloat16)
                ds = (p * (dp_ref[slot, :, cols] - stat_ref[2:3, cols])).astype(jnp.bfloat16)
                ds_ref[:, cols] = ds
                dq_ref[:, cols] += lax.dot_general(
                    keys, ds, tn, preferred_element_type=jnp.float32
                )
            dk = jnp.dot(ds_ref[...], q_ref[...], preferred_element_type=jnp.float32)
            dv = jnp.dot(p_ref[...], g_ref[...], preferred_element_type=jnp.float32)
            dkv_ref[slot, :, :HEAD_SIZE] = (dk * SCALE).astype(jnp.bfloat16)
            dkv_ref[slot, :, HEAD_SIZE:] = dv.astype(jnp.bfloat16)

        @pl.when(jnp.logical_not(need))
        def _():
            dkv_ref[slot] = jnp.zeros(dkv_ref.shape[1:], jnp.bfloat16)


def attention(info, rows, q_heads, g_heads, kv_slots, first):
    heads = kv_slots.shape[2] // (2 * HEAD_SIZE)
    tok = kv_slots.shape[1]
    wide = q_heads.shape[1]
    return pl.pallas_call(
        attention_kernel,
        grid=(heads,),
        in_specs=[
            pl.BlockSpec(memory_space=pltpu.SMEM),
            pl.BlockSpec((2, wide), lambda i: (0, 0)),
            pl.BlockSpec((None, wide, HEAD_SIZE), lambda i: (first + i, 0, 0)),
            pl.BlockSpec((None, wide, HEAD_SIZE), lambda i: (first + i, 0, 0)),
            pl.BlockSpec((REACH, tok, 2 * HEAD_SIZE), lambda i: (0, 0, i)),
        ],
        out_specs=[
            pl.BlockSpec((None, HEAD_SIZE, wide), lambda i: (i, 0, 0)),
            pl.BlockSpec((REACH, tok, 2 * HEAD_SIZE), lambda i: (0, 0, i)),
        ],
        out_shape=[
            jax.ShapeDtypeStruct((heads, HEAD_SIZE, wide), jnp.float32),
            jax.ShapeDtypeStruct(kv_slots.shape, jnp.bfloat16),
        ],
        scratch_shapes=[
            pltpu.VMEM((REACH, tok, wide), jnp.float32),
            pltpu.VMEM((REACH, tok, wide), jnp.float32),
            pltpu.VMEM((tok, wide), jnp.bfloat16),
            pltpu.VMEM((tok, wide), jnp.bfloat16),
            pltpu.VMEM((8, wide), jnp.float32),
        ],
        compiler_params=pltpu.CompilerParams(vmem_limit_bytes=56 * 1024 * 1024),
        cost_estimate=pl.CostEstimate(
            flops=heads * REACH * tok * wide * HEAD_SIZE * 20,
            bytes_accessed=heads * REACH * tok * HEAD_SIZE * 8,
            transcendentals=heads * REACH * tok * wide * 2,
        ),
    )(info, rows, q_heads, g_heads, kv_slots)


def shift(block, distance):
    devices = range(lax.axis_size("dc"))
    return lax.ppermute(
        block, "dc", [(i, i + distance) for i in devices if i + distance in devices]
    )


def swap(block, mask):
    return lax.ppermute(block, "dc", [(i, i ^ mask) for i in range(lax.axis_size("dc"))])


def shards(
    queries,
    keys,
    values,
    output_gradient,
    segment_ids,
    w_query,
    key_weight_matrix,
    value_weight_matrix,
):
    tok = queries.shape[0]
    kv_local = keys.shape[1] // HEAD_SIZE
    chunks = HEAD_CHUNKS if kv_local % HEAD_CHUNKS == 0 else 1
    wide = GROUP_WIDTH * tok
    me = lax.axis_index("dc")
    lane = lax.rem(me, PLANE)
    plane = me - lane
    f32 = jnp.float32

    pairs = jnp.concatenate(
        [keys.reshape(tok, kv_local, 1, HEAD_SIZE), values.reshape(tok, kv_local, 1, HEAD_SIZE)],
        axis=2,
    ).reshape(tok, chunks, -1)
    windows = []
    for c in range(chunks):
        own = pairs[:, c]
        near = shift(own, PLANE)
        far = shift(own, 2 * PLANE)
        slots = [own, near]
        for mask in range(1, PLANE):
            slots.append(swap(jnp.where(lane < (lane ^ mask), own, far), mask))
            slots.append(swap(near, mask))
        windows.append(jnp.stack(slots))

    bases = [me, me - PLANE]
    for mask in range(1, PLANE):
        other = lane ^ mask
        bases.append(jnp.where(other < lane, plane + other, plane - 2 * PLANE + other))
        bases.append(plane - PLANE + other)

    everyone = lax.all_gather(segment_ids, "dc", tiled=True)
    start = jnp.sum((everyone[None, :] < segment_ids[:, None]).astype(jnp.int32), axis=1)
    position = me * tok + jnp.arange(tok, dtype=jnp.int32)
    rows = jnp.tile(jnp.stack([start, position]), (1, GROUP_WIDTH))
    info = jnp.concatenate([jnp.stack(bases) * tok, start[:1], start[-1:]])

    def by_head(x):
        x = x.reshape(tok, kv_local, GROUP_WIDTH, HEAD_SIZE)
        return x.transpose(1, 2, 0, 3).reshape(kv_local, wide, HEAD_SIZE)

    q_heads = by_head(queries)
    g_heads = by_head(output_gradient)

    dq_parts = []
    totals = []
    per = kv_local // chunks
    for c in range(chunks):
        dq, parts = attention(info, rows, q_heads, g_heads, windows[c], c * per)
        dq_parts.append(dq)
        own = parts[0].astype(f32)
        near = parts[1].astype(f32)
        far = jnp.zeros_like(near)
        for mask in range(1, PLANE):
            back = swap(parts[2 * mask], mask).astype(f32)
            near = near + swap(parts[2 * mask + 1], mask).astype(f32)
            ahead = lane < (lane ^ mask)
            own = own + jnp.where(ahead, back, 0.0)
            far = far + jnp.where(ahead, 0.0, back)
        own = own + shift(near.astype(jnp.bfloat16), -PLANE).astype(f32)
        own = own + shift(far.astype(jnp.bfloat16), -2 * PLANE).astype(f32)
        totals.append(own.astype(jnp.bfloat16))
    total = jnp.concatenate(totals, axis=1).reshape(tok, kv_local, 2, HEAD_SIZE)
    key_grad = total[:, :, 0].reshape(tok, -1)
    value_grad = total[:, :, 1].reshape(tok, -1)
    dq = (jnp.concatenate(dq_parts, axis=0) * SCALE).astype(jnp.bfloat16)
    query_grad = (
        dq.reshape(kv_local, HEAD_SIZE, GROUP_WIDTH, tok).transpose(3, 0, 2, 1).reshape(tok, -1)
    )

    contract = (((1,), (1,)), ((), ()))
    dot = functools.partial(lax.dot_general, dimension_numbers=contract, preferred_element_type=f32)
    term = dot(query_grad, w_query)
    term = term + dot(key_grad, key_weight_matrix) + dot(value_grad, value_weight_matrix)
    term = term.astype(jnp.bfloat16)
    if lax.axis_size("kv") == 2:
        side = lax.axis_index("kv")
        half = term.shape[1] // 2
        mine = lax.dynamic_slice_in_dim(term, side * half, half, 1)
        theirs = lax.dynamic_slice_in_dim(term, (1 - side) * half, half, 1)
        got = lax.ppermute(theirs, "kv", [(0, 1), (1, 0)])
        input_grad = (mine.astype(f32) + got.astype(f32)).astype(jnp.bfloat16)
    else:
        input_grad = lax.psum_scatter(term, "kv", scatter_dimension=1, tiled=True)
    return (query_grad, key_grad, value_grad, input_grad)


def solution(mesh):
    in_specs = (
        P("dc", "kv"),
        P("dc", "kv"),
        P("dc", "kv"),
        P("dc", "kv"),
        P("dc"),
        P(None, "kv"),
        P(None, "kv"),
        P(None, "kv"),
    )
    out_specs = (P("dc", "kv"), P("dc", "kv"), P("dc", "kv"), P("dc", "kv"))
    return jax.shard_map(shards, mesh=mesh, in_specs=in_specs, out_specs=out_specs, check_vma=False)
```

```python
import functools

import jax
import jax.numpy as jnp
from jax import lax
from jax.experimental import pallas as pl
from jax.experimental.pallas import tpu as pltpu
from jax.sharding import PartitionSpec as P

QUERY_HEAD_COUNT = 40
KEY_VALUE_HEADS = 8
HEAD_SIZE = 128
GROUP_WIDTH = QUERY_HEAD_COUNT // KEY_VALUE_HEADS
REACH = 8
PLANE = 4
HEAD_CHUNKS = 2
SCALE = HEAD_SIZE ** (-0.5)
LOG2E = 1.4426950408889634
LOW = -1e30


def attention_kernel(
    info_ref, rows_ref, q_ref, g_ref, kv_ref, dq_ref, dkv_ref, s_ref, dp_ref, p_ref, ds_ref, stat_ref
):
    tok = kv_ref.shape[1]
    wide = q_ref.shape[0]
    lanes = []
    at = 0
    while at < wide:
        size = 512 if wide - at >= 1024 else wide - at
        lanes.append((at, size))
        at += size
    nt = (((1,), (1,)), ((), ()))
    tn = (((0,), (0,)), ((), ()))
    first_start = info_ref[REACH]
    last_start = info_ref[REACH + 1]

    stat_ref[0:1, :] = jnp.full((1, wide), LOW, jnp.float32)
    stat_ref[1:3, :] = jnp.zeros((2, wide), jnp.float32)

    def needed(slot):
        base = info_ref[slot]
        return (base >= 0) & (base + tok > first_start)

    def gather_stats(slot, masked):
        base = info_ref[slot]
        keys = kv_ref[slot, :, :HEAD_SIZE]
        values = kv_ref[slot, :, HEAD_SIZE:]
        for lo, size in lanes:
            cols = slice(lo, lo + size)
            s = lax.dot_general(
                keys, q_ref[cols, :], nt, preferred_element_type=jnp.float32
            ) * (SCALE * LOG2E)
            dp = lax.dot_general(values, g_ref[cols, :], nt, preferred_element_type=jnp.float32)
            if masked:
                pos = base + lax.broadcasted_iota(jnp.int32, (tok, size), 0)
                ok = (pos >= rows_ref[0:1, cols]) & (pos <= rows_ref[1:2, cols])
                s = jnp.where(ok, s, LOW)
            s_ref[slot, :, cols] = s
            dp_ref[slot, :, cols] = dp
            old = stat_ref[0:1, cols]
            new = jnp.maximum(old, jnp.max(s, axis=0, keepdims=True))
            fade = jnp.exp2(old - new)
            e = jnp.exp2(s - new)
            stat_ref[0:1, cols] = new
            stat_ref[1:2, cols] = stat_ref[1:2, cols] * fade + jnp.sum(e, axis=0, keepdims=True)
            stat_ref[2:3, cols] = stat_ref[2:3, cols] * fade + jnp.sum(
                e * dp, axis=0, keepdims=True
            )

    @pl.loop(0, REACH)
    def _(slot):
        whole = (slot > 0) & (info_ref[slot] >= last_start)

        @pl.when(needed(slot) & whole)
        def _():
            gather_stats(slot, False)

        @pl.when(needed(slot) & jnp.logical_not(whole))
        def _():
            gather_stats(slot, True)

    total = stat_ref[1:2, :]
    stat_ref[2:3, :] = stat_ref[2:3, :] / total
    stat_ref[0:1, :] = stat_ref[0:1, :] + jnp.log2(total)
    dq_ref[...] = jnp.zeros_like(dq_ref)

    @pl.loop(0, REACH)
    def _(slot):
        need = needed(slot)

        @pl.when(need)
        def _():
            keys = kv_ref[slot, :, :HEAD_SIZE]
            for lo, size in lanes:
                cols = slice(lo, lo + size)
                p = jnp.exp2(s_ref[slot, :, cols] - stat_ref[0:1, cols])
                p_ref[:, cols] = p.astype(jnp.bfloat16)
                ds = (p * (dp_ref[slot, :, cols] - stat_ref[2:3, cols])).astype(jnp.bfloat16)
                ds_ref[:, cols] = ds
                dq_ref[:, cols] += lax.dot_general(
                    keys, ds, tn, preferred_element_type=jnp.float32
                )
            dk = jnp.dot(ds_ref[...], q_ref[...], preferred_element_type=jnp.float32)
            dv = jnp.dot(p_ref[...], g_ref[...], preferred_element_type=jnp.float32)
            dkv_ref[slot, :, :HEAD_SIZE] = (dk * SCALE).astype(jnp.bfloat16)
            dkv_ref[slot, :, HEAD_SIZE:] = dv.astype(jnp.bfloat16)

        @pl.when(jnp.logical_not(need))
        def _():
            dkv_ref[slot] = jnp.zeros(dkv_ref.shape[1:], jnp.bfloat16)


def attention(info, rows, q_heads, g_heads, kv_slots, first):
    heads = kv_slots.shape[2] // (2 * HEAD_SIZE)
    tok = kv_slots.shape[1]
    wide = q_heads.shape[1]
    return pl.pallas_call(
        attention_kernel,
        grid=(heads,),
        in_specs=[
            pl.BlockSpec(memory_space=pltpu.SMEM),
            pl.BlockSpec((2, wide), lambda i: (0, 0)),
            pl.BlockSpec((None, wide, HEAD_SIZE), lambda i: (first + i, 0, 0)),
            pl.BlockSpec((None, wide, HEAD_SIZE), lambda i: (first + i, 0, 0)),
            pl.BlockSpec((REACH, tok, 2 * HEAD_SIZE), lambda i: (0, 0, i)),
        ],
        out_specs=[
            pl.BlockSpec((None, HEAD_SIZE, wide), lambda i: (i, 0, 0)),
            pl.BlockSpec((REACH, tok, 2 * HEAD_SIZE), lambda i: (0, 0, i)),
        ],
        out_shape=[
            jax.ShapeDtypeStruct((heads, HEAD_SIZE, wide), jnp.float32),
            jax.ShapeDtypeStruct(kv_slots.shape, jnp.bfloat16),
        ],
        scratch_shapes=[
            pltpu.VMEM((REACH, tok, wide), jnp.float32),
            pltpu.VMEM((REACH, tok, wide), jnp.float32),
            pltpu.VMEM((tok, wide), jnp.bfloat16),
            pltpu.VMEM((tok, wide), jnp.bfloat16),
            pltpu.VMEM((8, wide), jnp.float32),
        ],
        compiler_params=pltpu.CompilerParams(vmem_limit_bytes=56 * 1024 * 1024),
        cost_estimate=pl.CostEstimate(
            flops=heads * REACH * tok * wide * HEAD_SIZE * 20,
            bytes_accessed=heads * REACH * tok * HEAD_SIZE * 8,
            transcendentals=heads * REACH * tok * wide * 2,
        ),
    )(info, rows, q_heads, g_heads, kv_slots)


def shift(block, distance):
    devices = range(lax.axis_size("dc"))
    return lax.ppermute(
        block, "dc", [(i, i + distance) for i in devices if i + distance in devices]
    )


def swap(block, mask):
    return lax.ppermute(block, "dc", [(i, i ^ mask) for i in range(lax.axis_size("dc"))])


def shards(
    queries,
    keys,
    values,
    output_gradient,
    segment_ids,
    w_query,
    key_weight_matrix,
    value_weight_matrix,
):
    tok = queries.shape[0]
    kv_local = keys.shape[1] // HEAD_SIZE
    chunks = HEAD_CHUNKS if kv_local % HEAD_CHUNKS == 0 else 1
    wide = GROUP_WIDTH * tok
    me = lax.axis_index("dc")
    lane = lax.rem(me, PLANE)
    plane = me - lane
    f32 = jnp.float32

    pairs = jnp.concatenate(
        [keys.reshape(tok, kv_local, 1, HEAD_SIZE), values.reshape(tok, kv_local, 1, HEAD_SIZE)],
        axis=2,
    ).reshape(tok, chunks, -1)
    windows = []
    for c in range(chunks):
        own = pairs[:, c]
        near = shift(own, PLANE)
        far = shift(own, 2 * PLANE)
        slots = [own, near]
        for mask in range(1, PLANE):
            slots.append(swap(jnp.where(lane < (lane ^ mask), own, far), mask))
            slots.append(swap(near, mask))
        windows.append(jnp.stack(slots))

    bases = [me, me - PLANE]
    for mask in range(1, PLANE):
        other = lane ^ mask
        bases.append(jnp.where(other < lane, plane + other, plane - 2 * PLANE + other))
        bases.append(plane - PLANE + other)

    own_segs = segment_ids[None, :]
    near_segs = shift(own_segs, PLANE)
    far_segs = shift(own_segs, 2 * PLANE)
    seg_slots = [own_segs, near_segs]
    for mask in range(1, PLANE):
        first = jnp.where(lane < (lane ^ mask), own_segs, far_segs)
        seg_slots.append(swap(jnp.concatenate([first, near_segs]), mask))
    window_segs = jnp.concatenate(seg_slots)
    window_segs = jnp.where(jnp.stack(bases)[:, None] < 0, -1, window_segs).reshape(-1)
    earlier = (window_segs[None, :] < segment_ids[:, None]).astype(jnp.int32)
    start = (me - REACH + 1) * tok + jnp.sum(earlier, axis=1)
    position = me * tok + jnp.arange(tok, dtype=jnp.int32)
    rows = jnp.tile(jnp.stack([start, position]), (1, GROUP_WIDTH))
    info = jnp.concatenate([jnp.stack(bases) * tok, start[:1], start[-1:]])

    def by_head(x):
        x = x.reshape(tok, kv_local, GROUP_WIDTH, HEAD_SIZE)
        return x.transpose(1, 2, 0, 3).reshape(kv_local, wide, HEAD_SIZE)

    q_heads = by_head(queries)
    g_heads = by_head(output_gradient)

    dq_parts = []
    totals = []
    per = kv_local // chunks
    for c in range(chunks):
        dq, parts = attention(info, rows, q_heads, g_heads, windows[c], c * per)
        dq_parts.append(dq)
        own = parts[0].astype(f32)
        near = parts[1].astype(f32)
        far = jnp.zeros_like(near)
        for mask in range(1, PLANE):
            back = swap(parts[2 * mask], mask).astype(f32)
            near = near + swap(parts[2 * mask + 1], mask).astype(f32)
            ahead = lane < (lane ^ mask)
            own = own + jnp.where(ahead, back, 0.0)
            far = far + jnp.where(ahead, 0.0, back)
        own = own + shift(near.astype(jnp.bfloat16), -PLANE).astype(f32)
        own = own + shift(far.astype(jnp.bfloat16), -2 * PLANE).astype(f32)
        totals.append(own.astype(jnp.bfloat16))
    total = jnp.concatenate(totals, axis=1).reshape(tok, kv_local, 2, HEAD_SIZE)
    key_grad = total[:, :, 0].reshape(tok, -1)
    value_grad = total[:, :, 1].reshape(tok, -1)
    dq = (jnp.concatenate(dq_parts, axis=0) * SCALE).astype(jnp.bfloat16)
    query_grad = (
        dq.reshape(kv_local, HEAD_SIZE, GROUP_WIDTH, tok).transpose(3, 0, 2, 1).reshape(tok, -1)
    )

    contract = (((1,), (1,)), ((), ()))
    dot = functools.partial(lax.dot_general, dimension_numbers=contract, preferred_element_type=f32)
    term = dot(query_grad, w_query)
    term = term + dot(key_grad, key_weight_matrix) + dot(value_grad, value_weight_matrix)
    term = term.astype(jnp.bfloat16)
    if lax.axis_size("kv") == 2:
        side = lax.axis_index("kv")
        half = term.shape[1] // 2
        mine = lax.dynamic_slice_in_dim(term, side * half, half, 1)
        theirs = lax.dynamic_slice_in_dim(term, (1 - side) * half, half, 1)
        got = lax.ppermute(theirs, "kv", [(0, 1), (1, 0)])
        input_grad = (mine.astype(f32) + got.astype(f32)).astype(jnp.bfloat16)
    else:
        input_grad = lax.psum_scatter(term, "kv", scatter_dimension=1, tiled=True)
    return (query_grad, key_grad, value_grad, input_grad)


def solution(mesh):
    in_specs = (
        P("dc", "kv"),
        P("dc", "kv"),
        P("dc", "kv"),
        P("dc", "kv"),
        P("dc"),
        P(None, "kv"),
        P(None, "kv"),
        P(None, "kv"),
    )
    out_specs = (P("dc", "kv"), P("dc", "kv"), P("dc", "kv"), P("dc", "kv"))
    return jax.shard_map(shards, mesh=mesh, in_specs=in_specs, out_specs=out_specs, check_vma=False)
```

```python
import functools

import jax
import jax.numpy as jnp
from jax import lax
from jax.experimental import pallas as pl
from jax.experimental.pallas import tpu as pltpu
from jax.sharding import PartitionSpec as P

QUERY_HEAD_COUNT = 40
KEY_VALUE_HEADS = 8
HEAD_SIZE = 128
GROUP_WIDTH = QUERY_HEAD_COUNT // KEY_VALUE_HEADS
REACH = 8
PLANE = 4
HEAD_CHUNKS = 2
SCALE = HEAD_SIZE ** (-0.5)
LOG2E = 1.4426950408889634
LOW = -1e30


def attention_kernel(
    info_ref, rows_ref, q_ref, g_ref, kv_ref, dq_ref, dkv_ref, s_ref, dp_ref, p_ref, ds_ref, stat_ref
):
    tok = kv_ref.shape[1]
    wide = q_ref.shape[0]
    lanes = []
    at = 0
    while at < wide:
        size = 512 if wide - at >= 1024 else wide - at
        lanes.append((at, size))
        at += size
    nt = (((1,), (1,)), ((), ()))
    tn = (((0,), (0,)), ((), ()))
    first_start = info_ref[REACH]
    last_start = info_ref[REACH + 1]

    stat_ref[0:1, :] = jnp.full((1, wide), LOW, jnp.float32)
    stat_ref[1:3, :] = jnp.zeros((2, wide), jnp.float32)

    def needed(slot):
        base = info_ref[slot]
        return (base >= 0) & (base + tok > first_start)

    def gather_stats(slot, masked):
        base = info_ref[slot]
        keys = kv_ref[slot, :, :HEAD_SIZE]
        values = kv_ref[slot, :, HEAD_SIZE:]
        for lo, size in lanes:
            cols = slice(lo, lo + size)
            s = lax.dot_general(
                keys, q_ref[cols, :], nt, preferred_element_type=jnp.float32
            ) * (SCALE * LOG2E)
            dp = lax.dot_general(values, g_ref[cols, :], nt, preferred_element_type=jnp.float32)
            if masked:
                pos = base + lax.broadcasted_iota(jnp.int32, (tok, size), 0)
                ok = (pos >= rows_ref[0:1, cols]) & (pos <= rows_ref[1:2, cols])
                s = jnp.where(ok, s, LOW)
            s_ref[slot, :, cols] = s
            dp_ref[slot, :, cols] = dp
            old = stat_ref[0:1, cols]
            new = jnp.maximum(old, jnp.max(s, axis=0, keepdims=True))
            fade = jnp.exp2(old - new)
            e = jnp.exp2(s - new)
            stat_ref[0:1, cols] = new
            stat_ref[1:2, cols] = stat_ref[1:2, cols] * fade + jnp.sum(e, axis=0, keepdims=True)
            stat_ref[2:3, cols] = stat_ref[2:3, cols] * fade + jnp.sum(
                e * dp, axis=0, keepdims=True
            )

    @pl.loop(0, REACH)
    def _(slot):
        whole = (slot > 0) & (info_ref[slot] >= last_start)

        @pl.when(needed(slot) & whole)
        def _():
            gather_stats(slot, False)

        @pl.when(needed(slot) & jnp.logical_not(whole))
        def _():
            gather_stats(slot, True)

    total = stat_ref[1:2, :]
    stat_ref[2:3, :] = stat_ref[2:3, :] / total
    stat_ref[0:1, :] = stat_ref[0:1, :] + jnp.log2(total)
    dq_ref[...] = jnp.zeros_like(dq_ref)

    @pl.loop(0, REACH)
    def _(slot):
        need = needed(slot)

        @pl.when(need)
        def _():
            keys = kv_ref[slot, :, :HEAD_SIZE]
            for lo, size in lanes:
                cols = slice(lo, lo + size)
                p = jnp.exp2(s_ref[slot, :, cols] - stat_ref[0:1, cols])
                p_ref[:, cols] = p.astype(jnp.bfloat16)
                ds = (p * (dp_ref[slot, :, cols] - stat_ref[2:3, cols])).astype(jnp.bfloat16)
                ds_ref[:, cols] = ds
                dq_ref[:, cols] += lax.dot_general(
                    keys, ds, tn, preferred_element_type=jnp.float32
                )
            dk = jnp.dot(ds_ref[...], q_ref[...], preferred_element_type=jnp.float32)
            dv = jnp.dot(p_ref[...], g_ref[...], preferred_element_type=jnp.float32)
            dkv_ref[slot, :, :HEAD_SIZE] = (dk * SCALE).astype(jnp.bfloat16)
            dkv_ref[slot, :, HEAD_SIZE:] = dv.astype(jnp.bfloat16)

        @pl.when(jnp.logical_not(need))
        def _():
            dkv_ref[slot] = jnp.zeros(dkv_ref.shape[1:], jnp.bfloat16)


def attention(info, rows, q_heads, g_heads, kv_slots, first):
    heads = kv_slots.shape[2] // (2 * HEAD_SIZE)
    tok = kv_slots.shape[1]
    wide = q_heads.shape[1]
    return pl.pallas_call(
        attention_kernel,
        grid=(heads,),
        in_specs=[
            pl.BlockSpec(memory_space=pltpu.SMEM),
            pl.BlockSpec((2, wide), lambda i: (0, 0)),
            pl.BlockSpec((None, wide, HEAD_SIZE), lambda i: (first + i, 0, 0)),
            pl.BlockSpec((None, wide, HEAD_SIZE), lambda i: (first + i, 0, 0)),
            pl.BlockSpec((REACH, tok, 2 * HEAD_SIZE), lambda i: (0, 0, i)),
        ],
        out_specs=[
            pl.BlockSpec((None, HEAD_SIZE, wide), lambda i: (i, 0, 0)),
            pl.BlockSpec((REACH, tok, 2 * HEAD_SIZE), lambda i: (0, 0, i)),
        ],
        out_shape=[
            jax.ShapeDtypeStruct((heads, HEAD_SIZE, wide), jnp.float32),
            jax.ShapeDtypeStruct(kv_slots.shape, jnp.bfloat16),
        ],
        scratch_shapes=[
            pltpu.VMEM((REACH, tok, wide), jnp.float32),
            pltpu.VMEM((REACH, tok, wide), jnp.float32),
            pltpu.VMEM((tok, wide), jnp.bfloat16),
            pltpu.VMEM((tok, wide), jnp.bfloat16),
            pltpu.VMEM((8, wide), jnp.float32),
        ],
        compiler_params=pltpu.CompilerParams(vmem_limit_bytes=56 * 1024 * 1024),
        cost_estimate=pl.CostEstimate(
            flops=heads * REACH * tok * wide * HEAD_SIZE * 20,
            bytes_accessed=heads * REACH * tok * HEAD_SIZE * 8,
            transcendentals=heads * REACH * tok * wide * 2,
        ),
    )(info, rows, q_heads, g_heads, kv_slots)


def shift(block, distance):
    devices = range(lax.axis_size("dc"))
    return lax.ppermute(
        block, "dc", [(i, i + distance) for i in devices if i + distance in devices]
    )


def swap(block, mask):
    return lax.ppermute(block, "dc", [(i, i ^ mask) for i in range(lax.axis_size("dc"))])


def after(block, *arrived):
    wait = sum(x.reshape(-1)[0] * 0 for x in arrived)
    return block + wait


def shards(
    queries,
    keys,
    values,
    output_gradient,
    segment_ids,
    w_query,
    key_weight_matrix,
    value_weight_matrix,
):
    tok = queries.shape[0]
    kv_local = keys.shape[1] // HEAD_SIZE
    chunks = HEAD_CHUNKS if kv_local % HEAD_CHUNKS == 0 else 1
    wide = GROUP_WIDTH * tok
    me = lax.axis_index("dc")
    lane = lax.rem(me, PLANE)
    plane = me - lane
    f32 = jnp.float32

    pairs = jnp.concatenate(
        [keys.reshape(tok, kv_local, 1, HEAD_SIZE), values.reshape(tok, kv_local, 1, HEAD_SIZE)],
        axis=2,
    ).reshape(tok, chunks, -1)
    windows = []
    near = far = slots = None
    for c in range(chunks):
        own = pairs[:, c]
        if c:
            own = after(own, near, far)
        near = shift(own, PLANE)
        far = shift(own, 2 * PLANE)
        send_near, send_far = near, far
        if c:
            send_near, send_far = (after(x, *slots[2:]) for x in (near, far))
        slots = [own[None], near[None]]
        for mask in range(1, PLANE):
            first = jnp.where(lane < (lane ^ mask), own, send_far)
            slots.append(swap(jnp.stack([first, send_near]), mask))
        windows.append(jnp.concatenate(slots))

    bases = [me, me - PLANE]
    for mask in range(1, PLANE):
        other = lane ^ mask
        bases.append(jnp.where(other < lane, plane + other, plane - 2 * PLANE + other))
        bases.append(plane - PLANE + other)

    own_segs = segment_ids[None, :]
    near_segs = shift(own_segs, PLANE)
    far_segs = shift(own_segs, 2 * PLANE)
    seg_slots = [own_segs, near_segs]
    for mask in range(1, PLANE):
        first = jnp.where(lane < (lane ^ mask), own_segs, far_segs)
        seg_slots.append(swap(jnp.concatenate([first, near_segs]), mask))
    window_segs = jnp.concatenate(seg_slots)
    window_segs = jnp.where(jnp.stack(bases)[:, None] < 0, -1, window_segs).reshape(-1)
    earlier = (window_segs[None, :] < segment_ids[:, None]).astype(jnp.int32)
    start = (me - REACH + 1) * tok + jnp.sum(earlier, axis=1)
    position = me * tok + jnp.arange(tok, dtype=jnp.int32)
    rows = jnp.tile(jnp.stack([start, position]), (1, GROUP_WIDTH))
    info = jnp.concatenate([jnp.stack(bases) * tok, start[:1], start[-1:]])

    def by_head(x):
        x = x.reshape(tok, kv_local, GROUP_WIDTH, HEAD_SIZE)
        return x.transpose(1, 2, 0, 3).reshape(kv_local, wide, HEAD_SIZE)

    q_heads = by_head(queries)
    g_heads = by_head(output_gradient)

    dq_parts = []
    totals = []
    per = kv_local // chunks
    for c in range(chunks):
        dq, parts = attention(info, rows, q_heads, g_heads, windows[c], c * per)
        dq_parts.append(dq)
        own = parts[0].astype(f32)
        near = parts[1].astype(f32)
        far = jnp.zeros_like(near)
        for mask in range(1, PLANE):
            got = swap(parts[2 * mask : 2 * mask + 2], mask).astype(f32)
            back = got[0]
            near = near + got[1]
            ahead = lane < (lane ^ mask)
            own = own + jnp.where(ahead, back, 0.0)
            far = far + jnp.where(ahead, 0.0, back)
        own = own + shift(near.astype(jnp.bfloat16), -PLANE).astype(f32)
        own = own + shift(far.astype(jnp.bfloat16), -2 * PLANE).astype(f32)
        totals.append(own.astype(jnp.bfloat16))
    total = jnp.concatenate(totals, axis=1).reshape(tok, kv_local, 2, HEAD_SIZE)
    key_grad = total[:, :, 0].reshape(tok, -1)
    value_grad = total[:, :, 1].reshape(tok, -1)
    dq = (jnp.concatenate(dq_parts, axis=0) * SCALE).astype(jnp.bfloat16)
    query_grad = (
        dq.reshape(kv_local, HEAD_SIZE, GROUP_WIDTH, tok).transpose(3, 0, 2, 1).reshape(tok, -1)
    )

    contract = (((1,), (1,)), ((), ()))
    dot = functools.partial(lax.dot_general, dimension_numbers=contract, preferred_element_type=f32)
    term = dot(query_grad, w_query)
    term = term + dot(key_grad, key_weight_matrix) + dot(value_grad, value_weight_matrix)
    term = term.astype(jnp.bfloat16)
    if lax.axis_size("kv") == 2:
        side = lax.axis_index("kv")
        half = term.shape[1] // 2
        mine = lax.dynamic_slice_in_dim(term, side * half, half, 1)
        theirs = lax.dynamic_slice_in_dim(term, (1 - side) * half, half, 1)
        got = lax.ppermute(theirs, "kv", [(0, 1), (1, 0)])
        input_grad = (mine.astype(f32) + got.astype(f32)).astype(jnp.bfloat16)
    else:
        input_grad = lax.psum_scatter(term, "kv", scatter_dimension=1, tiled=True)
    return (query_grad, key_grad, value_grad, input_grad)


def solution(mesh):
    in_specs = (
        P("dc", "kv"),
        P("dc", "kv"),
        P("dc", "kv"),
        P("dc", "kv"),
        P("dc"),
        P(None, "kv"),
        P(None, "kv"),
        P(None, "kv"),
    )
    out_specs = (P("dc", "kv"), P("dc", "kv"), P("dc", "kv"), P("dc", "kv"))
    return jax.shard_map(shards, mesh=mesh, in_specs=in_specs, out_specs=out_specs, check_vma=False)
```

```python
import functools

import jax
import jax.numpy as jnp
from jax import lax
from jax.experimental import pallas as pl
from jax.experimental.pallas import tpu as pltpu
from jax.sharding import PartitionSpec as P

QUERY_HEAD_COUNT = 40
KEY_VALUE_HEADS = 8
HEAD_SIZE = 128
GROUP_WIDTH = QUERY_HEAD_COUNT // KEY_VALUE_HEADS
REACH = 8
PLANE = 4
SCALE = HEAD_SIZE ** (-0.5)
LOG2E = 1.4426950408889634
LOW = -1e30


def attention_kernel(
    info_ref, rows_ref, q_ref, g_ref, kv_ref, dq_ref, dkv_ref, s_ref, dp_ref, p_ref, ds_ref, stat_ref
):
    tok = kv_ref.shape[1]
    wide = q_ref.shape[0]
    lanes = []
    at = 0
    while at < wide:
        size = 512 if wide - at >= 1024 else wide - at
        lanes.append((at, size))
        at += size
    nt = (((1,), (1,)), ((), ()))
    tn = (((0,), (0,)), ((), ()))
    first_start = info_ref[REACH]
    last_start = info_ref[REACH + 1]

    stat_ref[0:1, :] = jnp.full((1, wide), LOW, jnp.float32)
    stat_ref[1:3, :] = jnp.zeros((2, wide), jnp.float32)

    def needed(slot):
        base = info_ref[slot]
        return (base >= 0) & (base + tok > first_start)

    def gather_stats(slot, masked):
        base = info_ref[slot]
        keys = kv_ref[slot, :, :HEAD_SIZE]
        values = kv_ref[slot, :, HEAD_SIZE:]
        for lo, size in lanes:
            cols = slice(lo, lo + size)
            s = lax.dot_general(
                keys, q_ref[cols, :], nt, preferred_element_type=jnp.float32
            ) * (SCALE * LOG2E)
            dp = lax.dot_general(values, g_ref[cols, :], nt, preferred_element_type=jnp.float32)
            if masked:
                pos = base + lax.broadcasted_iota(jnp.int32, (tok, size), 0)
                ok = (pos >= rows_ref[0:1, cols]) & (pos <= rows_ref[1:2, cols])
                s = jnp.where(ok, s, LOW)
            s_ref[slot, :, cols] = s
            dp_ref[slot, :, cols] = dp
            old = stat_ref[0:1, cols]
            new = jnp.maximum(old, jnp.max(s, axis=0, keepdims=True))
            fade = jnp.exp2(old - new)
            e = jnp.exp2(s - new)
            stat_ref[0:1, cols] = new
            stat_ref[1:2, cols] = stat_ref[1:2, cols] * fade + jnp.sum(e, axis=0, keepdims=True)
            stat_ref[2:3, cols] = stat_ref[2:3, cols] * fade + jnp.sum(
                e * dp, axis=0, keepdims=True
            )

    @pl.loop(0, REACH)
    def _(slot):
        whole = (slot > 0) & (info_ref[slot] >= last_start)

        @pl.when(needed(slot) & whole)
        def _():
            gather_stats(slot, False)

        @pl.when(needed(slot) & jnp.logical_not(whole))
        def _():
            gather_stats(slot, True)

    total = stat_ref[1:2, :]
    stat_ref[2:3, :] = stat_ref[2:3, :] / total
    stat_ref[0:1, :] = stat_ref[0:1, :] + jnp.log2(total)
    dq_ref[...] = jnp.zeros_like(dq_ref)

    @pl.loop(0, REACH)
    def _(slot):
        need = needed(slot)

        @pl.when(need)
        def _():
            keys = kv_ref[slot, :, :HEAD_SIZE]
            for lo, size in lanes:
                cols = slice(lo, lo + size)
                p = jnp.exp2(s_ref[slot, :, cols] - stat_ref[0:1, cols])
                p_ref[:, cols] = p.astype(jnp.bfloat16)
                ds = (p * (dp_ref[slot, :, cols] - stat_ref[2:3, cols])).astype(jnp.bfloat16)
                ds_ref[:, cols] = ds
                dq_ref[:, cols] += lax.dot_general(
                    keys, ds, tn, preferred_element_type=jnp.float32
                )
            dk = jnp.dot(ds_ref[...], q_ref[...], preferred_element_type=jnp.float32)
            dv = jnp.dot(p_ref[...], g_ref[...], preferred_element_type=jnp.float32)
            dkv_ref[slot, :, :HEAD_SIZE] = (dk * SCALE).astype(jnp.bfloat16)
            dkv_ref[slot, :, HEAD_SIZE:] = dv.astype(jnp.bfloat16)

        @pl.when(jnp.logical_not(need))
        def _():
            dkv_ref[slot] = jnp.zeros(dkv_ref.shape[1:], jnp.bfloat16)


def attention(info, rows, q_heads, g_heads, kv_slots, first):
    heads = kv_slots.shape[2] // (2 * HEAD_SIZE)
    tok = kv_slots.shape[1]
    wide = q_heads.shape[1]
    return pl.pallas_call(
        attention_kernel,
        grid=(heads,),
        in_specs=[
            pl.BlockSpec(memory_space=pltpu.SMEM),
            pl.BlockSpec((2, wide), lambda i: (0, 0)),
            pl.BlockSpec((None, wide, HEAD_SIZE), lambda i: (first + i, 0, 0)),
            pl.BlockSpec((None, wide, HEAD_SIZE), lambda i: (first + i, 0, 0)),
            pl.BlockSpec((REACH, tok, 2 * HEAD_SIZE), lambda i: (0, 0, i)),
        ],
        out_specs=[
            pl.BlockSpec((None, HEAD_SIZE, wide), lambda i: (i, 0, 0)),
            pl.BlockSpec((REACH, tok, 2 * HEAD_SIZE), lambda i: (0, 0, i)),
        ],
        out_shape=[
            jax.ShapeDtypeStruct((heads, HEAD_SIZE, wide), jnp.float32),
            jax.ShapeDtypeStruct(kv_slots.shape, jnp.bfloat16),
        ],
        scratch_shapes=[
            pltpu.VMEM((REACH, tok, wide), jnp.float32),
            pltpu.VMEM((REACH, tok, wide), jnp.float32),
            pltpu.VMEM((tok, wide), jnp.bfloat16),
            pltpu.VMEM((tok, wide), jnp.bfloat16),
            pltpu.VMEM((8, wide), jnp.float32),
        ],
        compiler_params=pltpu.CompilerParams(vmem_limit_bytes=56 * 1024 * 1024),
        cost_estimate=pl.CostEstimate(
            flops=heads * REACH * tok * wide * HEAD_SIZE * 20,
            bytes_accessed=heads * REACH * tok * HEAD_SIZE * 8,
            transcendentals=heads * REACH * tok * wide * 2,
        ),
    )(info, rows, q_heads, g_heads, kv_slots)


def shift(block, distance):
    devices = range(lax.axis_size("dc"))
    return lax.ppermute(
        block, "dc", [(i, i + distance) for i in devices if i + distance in devices]
    )


def swap(block, mask):
    return lax.ppermute(block, "dc", [(i, i ^ mask) for i in range(lax.axis_size("dc"))])


def after(block, *arrived):
    wait = sum(x.reshape(-1)[0] * 0 for x in arrived)
    return block + wait


def shards(
    queries,
    keys,
    values,
    output_gradient,
    segment_ids,
    w_query,
    key_weight_matrix,
    value_weight_matrix,
):
    tok = queries.shape[0]
    kv_local = keys.shape[1] // HEAD_SIZE
    sizes = [1, 1, 2] if kv_local == 4 else [kv_local]
    chunks = len(sizes)
    firsts = [sum(sizes[:c]) for c in range(chunks)]
    wide = GROUP_WIDTH * tok
    me = lax.axis_index("dc")
    lane = lax.rem(me, PLANE)
    plane = me - lane
    f32 = jnp.float32

    pairs = jnp.concatenate(
        [keys.reshape(tok, kv_local, 1, HEAD_SIZE), values.reshape(tok, kv_local, 1, HEAD_SIZE)],
        axis=2,
    ).reshape(tok, -1)
    windows = []
    levels = []
    near = far = slots = None
    for c in range(chunks):
        lo = firsts[c] * 2 * HEAD_SIZE
        own = pairs[:, lo : lo + sizes[c] * 2 * HEAD_SIZE]
        if c:
            own = after(own, near, far)
        near = shift(own, PLANE)
        far = shift(own, 2 * PLANE)
        levels.append((near, far))
        send_near, send_far = near, far
        if c:
            send_near, send_far = (after(x, *slots[2:]) for x in (near, far))
        slots = [own[None], near[None]]
        for mask in range(1, PLANE):
            first = jnp.where(lane < (lane ^ mask), own, send_far)
            slots.append(swap(jnp.stack([first, send_near]), mask))
        windows.append(jnp.concatenate(slots))

    bases = [me, me - PLANE]
    for mask in range(1, PLANE):
        other = lane ^ mask
        bases.append(jnp.where(other < lane, plane + other, plane - 2 * PLANE + other))
        bases.append(plane - PLANE + other)

    own_segs = segment_ids[None, :]
    near_segs = shift(own_segs, PLANE)
    far_segs = shift(own_segs, 2 * PLANE)
    seg_slots = [own_segs, near_segs]
    for mask in range(1, PLANE):
        first = jnp.where(lane < (lane ^ mask), own_segs, far_segs)
        seg_slots.append(swap(jnp.concatenate([first, near_segs]), mask))
    window_segs = jnp.concatenate(seg_slots)
    window_segs = jnp.where(jnp.stack(bases)[:, None] < 0, -1, window_segs).reshape(-1)
    earlier = (window_segs[None, :] < segment_ids[:, None]).astype(jnp.int32)
    start = (me - REACH + 1) * tok + jnp.sum(earlier, axis=1)
    position = me * tok + jnp.arange(tok, dtype=jnp.int32)
    rows = jnp.tile(jnp.stack([start, position]), (1, GROUP_WIDTH))
    info = jnp.concatenate([jnp.stack(bases) * tok, start[:1], start[-1:]])

    def by_head(x):
        x = x.reshape(tok, kv_local, GROUP_WIDTH, HEAD_SIZE)
        return x.transpose(1, 2, 0, 3).reshape(kv_local, wide, HEAD_SIZE)

    q_heads = by_head(queries)
    g_heads = by_head(output_gradient)

    dq_parts = []
    totals = []
    for c in range(chunks):
        ready = info
        if c + 1 < chunks:
            ready = ready + sum(x[0, 0] * 0 for x in levels[c + 1]).astype(jnp.int32)
        dq, parts = attention(ready, rows, q_heads, g_heads, windows[c], firsts[c])
        dq_parts.append(dq)
        own = parts[0].astype(f32)
        near = parts[1].astype(f32)
        far = jnp.zeros_like(near)
        for mask in range(1, PLANE):
            got = swap(parts[2 * mask : 2 * mask + 2], mask).astype(f32)
            back = got[0]
            near = near + got[1]
            ahead = lane < (lane ^ mask)
            own = own + jnp.where(ahead, back, 0.0)
            far = far + jnp.where(ahead, 0.0, back)
        own = own + shift(near.astype(jnp.bfloat16), -PLANE).astype(f32)
        own = own + shift(far.astype(jnp.bfloat16), -2 * PLANE).astype(f32)
        totals.append(own.astype(jnp.bfloat16))
    total = jnp.concatenate(totals, axis=1).reshape(tok, kv_local, 2, HEAD_SIZE)
    key_grad = total[:, :, 0].reshape(tok, -1)
    value_grad = total[:, :, 1].reshape(tok, -1)
    dq = (jnp.concatenate(dq_parts, axis=0) * SCALE).astype(jnp.bfloat16)
    query_grad = (
        dq.reshape(kv_local, HEAD_SIZE, GROUP_WIDTH, tok).transpose(3, 0, 2, 1).reshape(tok, -1)
    )

    contract = (((1,), (1,)), ((), ()))
    dot = functools.partial(lax.dot_general, dimension_numbers=contract, preferred_element_type=f32)
    term = dot(query_grad, w_query)
    term = term + dot(key_grad, key_weight_matrix) + dot(value_grad, value_weight_matrix)
    term = term.astype(jnp.bfloat16)
    if lax.axis_size("kv") == 2:
        side = lax.axis_index("kv")
        half = term.shape[1] // 2
        mine = lax.dynamic_slice_in_dim(term, side * half, half, 1)
        theirs = lax.dynamic_slice_in_dim(term, (1 - side) * half, half, 1)
        got = lax.ppermute(theirs, "kv", [(0, 1), (1, 0)])
        input_grad = (mine.astype(f32) + got.astype(f32)).astype(jnp.bfloat16)
    else:
        input_grad = lax.psum_scatter(term, "kv", scatter_dimension=1, tiled=True)
    return (query_grad, key_grad, value_grad, input_grad)


def solution(mesh):
    in_specs = (
        P("dc", "kv"),
        P("dc", "kv"),
        P("dc", "kv"),
        P("dc", "kv"),
        P("dc"),
        P(None, "kv"),
        P(None, "kv"),
        P(None, "kv"),
    )
    out_specs = (P("dc", "kv"), P("dc", "kv"), P("dc", "kv"), P("dc", "kv"))
    return jax.shard_map(shards, mesh=mesh, in_specs=in_specs, out_specs=out_specs, check_vma=False)
```
